32 devices in a mesh: group: 2 (over y), seq: 8 (over z, x), head: 2 (over core).
Axes of the slice: x: 2, y: 2, z: 4, core: 2. Of those that a mesh axis runs over, the one named last changes fastest.
Arguments:
- x_stream: bfloat16 [2048, 4096], P(('group', 'seq'), 'head'), parts along dimension 0, may hold values from -6 to 6
- z_stream: bfloat16 [2048, 4096], P(('group', 'seq'), 'head'), parts along dimension 0, may hold values from -6 to 6
- b_stream: bfloat16 [2048, 1024], P(('group', 'seq'), 'head'), parts along dimension 0, may hold values from -6 to 6
- c_stream: bfloat16 [2048, 1024], P(('group', 'seq'), 'head'), parts along dimension 0, may hold values from -6 to 6
- dt_raw: float32 [128, 2048], P('head', ('group', 'seq')), parts along dimension 1, may hold values from -6 to 4
- a_log: float32 [256], P(('group', 'head')), parts along dimension 0, may hold values from -10 to 0
- skip_coef: float32 [128], P('head'), may hold values from 0.5 to 2
- conv_x: float32 [4, 4096], P(None, 'head'), may hold values from -3 to 3
- conv_b: float32 [4, 1024], P(None, 'head'), may hold values from -3 to 3
- conv_c: float32 [4, 1024], P(None, 'head'), may hold values from -3 to 3
- norm_gain: float32 [4096], P('head'), may hold values from 0.1 to 1.9
- state_in: float32 [256, 32, 128], P(('group', 'head')), parts along dimension 0, may hold values from -6 to 6
- grad_out: bfloat16 [2048, 4096], P(('group', 'seq'), 'head'), parts along dimension 0, may hold values from -6 to 6
Outputs:
- grad_x: bfloat16 [2048, 4096], P(('group', 'seq'), 'head'), parts along dimension 0
- grad_z: bfloat16 [2048, 4096], P(('group', 'seq'), 'head'), parts along dimension 0
- grad_b: bfloat16 [2048, 1024], P(('group', 'seq'), 'head'), parts along dimension 0
- grad_c: bfloat16 [2048, 1024], P(('group', 'seq'), 'head'), parts along dimension 0
- grad_dt: float32 [128, 2048], P('head', ('group', 'seq')), parts along dimension 1
The draws below stay inside these ranges and needn't reach their ends.
There are 2 independent parts, one for each index of `group`. The reference program is written for one: setup_inputs(seed, part) draws one part's arguments, and reference() takes and returns one part's arrays. A program takes and returns all parts, laid end to end along the dimension named above; an argument that names none is the same for every part. Nothing has to cross between parts.
All inputs are finite; a program needn't handle non-finite values.
Results may differ from the reference program's by a relative error of at most 0.001.
Values may be sent and summed in bfloat16 or wider, within the bound.
A program may use at most 128 MiB of HBM per device.

```python
import math
import jax
import jax.numpy as jnp
from jax import lax

H = 128
P_SIZE = 32
N = 128
G = 8
K = 4
TOK_DEV = 128
TOKENS = 1024


def decay_plan(key):
    base_key = jax.random.fold_in(key, 7)
    key_fast, key_rate, key_slow, key_rough, key_block = jax.random.split(base_key, 5)
    fast_share = 0.5
    lowest = 0.3
    highest = 2.0
    fast_heads = jax.random.uniform(key_fast, (H,), jnp.float32) < fast_share
    fast_rate = jnp.exp(jax.random.uniform(key_rate, (H,), jnp.float32, math.log(1.0 / 50.0), math.log(1.0 / 30.0)))
    slow_total = jnp.exp(jax.random.uniform(key_slow, (H,), jnp.float32, math.log(lowest), math.log(highest)))
    slow_rate = jnp.minimum(slow_total / (TOKENS * 0.02), 1.0)
    slow_unit = slow_total / (TOKENS * slow_rate)
    step_unit = jnp.where(fast_heads, 1.0, slow_unit)
    head_rates = jnp.where(fast_heads, fast_rate, slow_rate)
    roughness = jnp.exp(jax.random.uniform(key_rough, (H, TOKENS), jnp.float32, math.log(0.5), math.log(2.0)))
    block_count = TOKENS // TOK_DEV
    block_factor = jnp.exp(jax.random.uniform(key_block, (H, block_count), jnp.float32, math.log(0.5), math.log(2.0)))
    block_spread = jnp.repeat(block_factor, TOK_DEV, axis=1)
    step_target = step_unit[:, None] * roughness * block_spread
    raw_steps = step_target + jnp.log(-jnp.expm1(-step_target))
    return (jnp.minimum(jnp.log(head_rates), 0.0).astype(jnp.float32), raw_steps.astype(jnp.float32))


def draw_a_log(key, part):
    return decay_plan(key)[0]


def draw_dt_raw(key, part):
    return decay_plan(key)[1]


def steps_of(own_key, shape, cuts, least, high):
    factor_of = 1.0
    for dim, parts in cuts:
        heights = jax.random.uniform(jax.random.fold_in(jax.random.fold_in(own_key, 6), dim), (parts,), jnp.float32, least / len(cuts), high / len(cuts))
        factor_of = factor_of * jnp.repeat(jnp.exp(heights), shape[dim] // parts).reshape((-1,) + (1,) * (len(shape) - 1 - dim))
    return factor_of


def bell_draw(own_key, dims, spread, limit, cuts=(), held_as=jnp.bfloat16):
    factor_of = steps_of(own_key, dims, cuts, -0.22, 0.18) if cuts else 1.0
    array = jax.random.normal(own_key, dims, jnp.float32) * spread * factor_of
    return jnp.minimum(jnp.maximum(array, -limit), limit).astype(held_as)


def setup_inputs(seed: int = 0, part: int = 0) -> dict:
    key_list = jax.random.split(jax.random.key(seed), 14)
    own_keys = jax.random.split(jax.random.fold_in(key_list[13], part), 14)
    x_stream = bell_draw(own_keys[0], (TOKENS, H * P_SIZE), 1.0, 6.0, ((0, 8), (1, 2)))
    z_stream = bell_draw(own_keys[1], (TOKENS, H * P_SIZE), 1.0, 6.0, ((0, 8), (1, 2)))
    b_stream = bell_draw(own_keys[2], (TOKENS, G * N), 1.0, 6.0, ((0, 8), (1, 2)))
    c_stream = bell_draw(own_keys[3], (TOKENS, G * N), 1.0, 6.0, ((0, 8), (1, 2)))
    dt_raw = draw_dt_raw(jax.random.fold_in(jax.random.fold_in(key_list[13], part), 71), part)
    a_log = draw_a_log(jax.random.fold_in(jax.random.fold_in(key_list[13], part), 71), part)
    skip_coef = jnp.clip(0.5 + 1.5 * jax.random.uniform(key_list[6], (H,), jnp.float32) ** steps_of(key_list[6], (H,), ((0, 2),), -0.2, 0.2), 0.5, 2.0)
    conv_x = bell_draw(key_list[7], (K, H * P_SIZE), K ** -0.5, 3.0, ((1, 2),), jnp.float32)
    conv_b = bell_draw(key_list[8], (K, G * N), K ** -0.5, 3.0, ((1, 2),), jnp.float32)
    conv_c = bell_draw(key_list[9], (K, G * N), K ** -0.5, 3.0, ((1, 2),), jnp.float32)
    norm_gain = jnp.clip(1.0 + 0.18 * jax.random.normal(key_list[10], (H * P_SIZE,), jnp.float32), 0.1, 1.9)
    state_in = bell_draw(own_keys[11], (H, P_SIZE, N), 1.0, 6.0, ((0, 2),), jnp.float32)
    grad_out = bell_draw(own_keys[12], (TOKENS, H * P_SIZE), 1.0, 6.0, ((0, 8), (1, 2)))
    return {"x_stream": x_stream, "z_stream": z_stream, "b_stream": b_stream, "c_stream": c_stream, "dt_raw": dt_raw, "a_log": a_log, "skip_coef": skip_coef, "conv_x": conv_x, "conv_b": conv_b, "conv_c": conv_c, "norm_gain": norm_gain, "state_in": state_in, "grad_out": grad_out}


EPS = 1e-05
EXACT = lax.Precision.HIGHEST

def causal_conv(edge_rows, values, weight):
    width = weight.shape[0]
    length = values.shape[0]
    joined = jnp.concatenate([edge_rows.astype(jnp.float32), values.astype(jnp.float32)], axis=0)
    summed = jnp.zeros((length, values.shape[1]), jnp.float32)
    for offset in range(width):
        summed = summed + weight[offset][None, :] * joined[offset:offset + length]
    return summed

def activate(pre_x, pre_b, pre_c, dt_raw, a_log):
    signal = jax.nn.silu(pre_x)
    b_coef = jax.nn.silu(pre_b)
    c_coef = jax.nn.silu(pre_c)
    steps = jax.nn.softplus(dt_raw)
    rates = -jnp.exp(a_log)[:, None] * steps
    cumulative = jnp.cumsum(rates, axis=1)
    return (signal, b_coef, c_coef, steps, cumulative)

def block_summary(signal, b_coef, steps, cumulative, group_count):
    length = signal.shape[0]
    head_count = steps.shape[0]
    per_group = head_count // group_count
    head_dim = signal.shape[1] // head_count
    state_width = b_coef.shape[1] // group_count
    weights = jnp.exp(cumulative[:, -1:] - cumulative) * steps
    scaled = signal.reshape(length, group_count, per_group, head_dim) * weights.T.reshape(length, group_count, per_group)[..., None]
    b_groups = b_coef.reshape(length, group_count, state_width)
    summary = jnp.einsum('tgjp,tgn->gjpn', scaled, b_groups, precision=EXACT)
    return (jnp.exp(cumulative[:, -1]), summary.reshape(head_count, head_dim, state_width))

def block_output(signal, b_coef, c_coef, steps, cumulative, entering, gate_rows, skip_coef, norm_gain, group_count):
    length = signal.shape[0]
    head_count = steps.shape[0]
    per_group = head_count // group_count
    head_dim = signal.shape[1] // head_count
    state_width = b_coef.shape[1] // group_count
    b_groups = b_coef.reshape(length, group_count, state_width)
    c_groups = c_coef.reshape(length, group_count, state_width)
    scores = jnp.einsum('tgn,rgn->gtr', c_groups, b_groups, precision=EXACT)
    causal = jnp.arange(length)[:, None] >= jnp.arange(length)[None, :]
    log_gaps = cumulative[:, :, None] - cumulative[:, None, :]
    mask_decay = jnp.exp(jnp.where(causal[None], log_gaps, -jnp.inf)).reshape(group_count, per_group, length, length)
    mixing = scores[:, None] * mask_decay
    inputs_x = signal.reshape(length, group_count, per_group, head_dim)
    scaled = inputs_x * steps.T.reshape(length, group_count, per_group)[..., None]
    within = jnp.einsum('gjtr,rgjp->tgjp', mixing, scaled, precision=EXACT)
    carried = jnp.einsum('tgn,gjpn->tgjp', c_groups, entering.reshape(group_count, per_group, head_dim, state_width), precision=EXACT)
    carried = carried * jnp.exp(cumulative).T.reshape(length, group_count, per_group)[..., None]
    mixed = within + carried + skip_coef.reshape(group_count, per_group)[None, :, :, None] * inputs_x
    gated = mixed * jax.nn.silu(gate_rows.reshape(length, group_count, per_group, head_dim))
    inv_rms = lax.rsqrt(lax.optimization_barrier(jnp.mean(gated * gated, axis=(2, 3), keepdims=True)) + EPS)
    return (gated * inv_rms).reshape(length, head_count * head_dim) * norm_gain[None, :]

def reference(x_stream, z_stream, b_stream, c_stream, dt_raw, a_log, skip_coef, conv_x, conv_b, conv_c, norm_gain, state_in, grad_out):
    block_count = TOKENS // TOK_DEV
    edge = K - 1

    def forward(x_full, z_full, b_full, c_full, raw_full):
        x_blocks = x_full.reshape(block_count, TOK_DEV, H * P_SIZE)
        z_blocks = z_full.reshape(block_count, TOK_DEV, H * P_SIZE)
        b_blocks = b_full.reshape(block_count, TOK_DEV, G * N)
        c_blocks = c_full.reshape(block_count, TOK_DEV, G * N)
        raw_blocks = raw_full.reshape(H, block_count, TOK_DEV).transpose(1, 0, 2)

        @jax.checkpoint
        def advance(carry, block):
            state, tail_x, tail_b, tail_c = carry
            x_block, z_block, b_block, c_block, raw_block = block
            pre_x = causal_conv(tail_x, x_block, conv_x)
            pre_b = causal_conv(tail_b, b_block, conv_b)
            pre_c = causal_conv(tail_c, c_block, conv_c)
            signal, b_coef, c_coef, steps, cumulative = activate(pre_x, pre_b, pre_c, raw_block, a_log)
            normed = block_output(signal, b_coef, c_coef, steps, cumulative, state, z_block, skip_coef, norm_gain, G)
            decay, summary = block_summary(signal, b_coef, steps, cumulative, G)
            new_state = decay[:, None, None] * state + summary
            return ((new_state, x_block[-edge:], b_block[-edge:], c_block[-edge:]), normed)
        start = (state_in, jnp.zeros((edge, H * P_SIZE), jnp.float32), jnp.zeros((edge, G * N), jnp.float32), jnp.zeros((edge, G * N), jnp.float32))
        final, outputs = lax.scan(advance, start, (x_blocks, z_blocks, b_blocks, c_blocks, raw_blocks))
        return outputs.reshape(TOKENS, H * P_SIZE)
    primal, backward = jax.vjp(forward, x_stream.astype(jnp.float32), z_stream.astype(jnp.float32), b_stream.astype(jnp.float32), c_stream.astype(jnp.float32), dt_raw)
    grad_xf, grad_zf, grad_bf, grad_cf, grad_raw = backward(grad_out.astype(jnp.float32))
    return (grad_xf.astype(jnp.bfloat16), grad_zf.astype(jnp.bfloat16), grad_bf.astype(jnp.bfloat16), grad_cf.astype(jnp.bfloat16), grad_raw)
```

```python
import functools

import jax
import jax.numpy as jnp
from jax import lax
from jax.experimental import pallas as pl
from jax.experimental.pallas import tpu as pltpu
from jax.sharding import PartitionSpec as P

EPS = 1e-05
EXACT = lax.Precision.HIGHEST
MESH = pl.DeviceIdType.MESH
F32, BF16 = jnp.float32, jnp.bfloat16
NN, NT, TN = (((1,), (0,)), ((1,), (1,)), ((0,), (0,)))
BLOCK = 4


def split(a):
    high = a.astype(BF16)
    return high, (a - high.astype(F32)).astype(BF16)


def dot(a, b, dims):
    return lax.dot_general(a, b, (dims, ((), ())), preferred_element_type=F32)


def dot3(a, b, dims):
    (ah, al), (bh, bl) = a, b
    return dot(ah, bh, dims) + (dot(ah, bl, dims) + dot(al, bh, dims))


def exact(a, b, dims=NN):
    return lax.dot_general(a, b, (dims, ((), ())), precision=EXACT, preferred_element_type=F32)


def iota(shape, dim):
    return lax.broadcasted_iota(jnp.int32, shape, dim)


def sigmoid(v):
    return 1.0 / (1.0 + jnp.exp(-v))


def kernel(
    x_ref, z_ref, b_ref, c_ref, dt_ref, alog_ref, skip_ref, wx_ref, wb_ref, wc_ref, gain_ref, state_ref, go_ref,
    gx_ref, gz_ref, gb_ref, gc_ref, gdt_ref,
    halo_x, halo_b, halo_c, ext, pre_x, pre_b, pre_c, sig, bco, cco, step_row, cum_row, acol, skcol, cum_t,
    step_x, ecum_x, e_x, dec_x, summ, ent, exi, d_ent, d_exi, back, dm_s, r1_s, dsc_s, dbs, dcs, mask_s,
    gp, ghalo, gsend, gpb,
    hs_sem, hr_sem, fs_sem, fr_sem, bs_sem, br_sem, gs_sem, gr_sem,
):
    me, peers = lax.axis_index("seq"), lax.axis_size("seq")
    first, last = me == 0, me == peers - 1
    tok, chan = x_ref.shape
    heads = dt_ref.shape[0]
    hd = chan // heads
    nn = state_ref.shape[1]
    groups = b_ref.shape[1] // nn
    per = heads // groups
    gw = chan // groups
    bw = BLOCK * hd
    blocks = gw // bw
    taps = wx_ref.shape[0]
    chunks = groups * blocks
    before, after = {"seq": jnp.maximum(me - 1, 0)}, {"seq": jnp.minimum(me + 1, peers - 1)}

    barrier = pltpu.get_barrier_semaphore()

    @pl.when(jnp.logical_not(first))
    def _():
        pl.semaphore_signal(barrier, inc=1, device_id=before, device_id_type=MESH)

    @pl.when(jnp.logical_not(last))
    def _():
        pl.semaphore_signal(barrier, inc=1, device_id=after, device_id_type=MESH)

    pl.semaphore_wait(barrier, jnp.minimum(me, 1) + jnp.minimum(peers - 1 - me, 1))

    def remote(src, dst, ssem, rsem, to):
        return pltpu.make_async_remote_copy(
            src_ref=src, dst_ref=dst, send_sem=ssem, recv_sem=rsem, device_id=to, device_id_type=MESH
        )

    halos = [
        remote(src.at[pl.ds(tok - 16, 16), :], dst, hs_sem.at[i], hr_sem.at[i], after)
        for i, (src, dst) in enumerate(((x_ref, halo_x), (b_ref, halo_b), (c_ref, halo_c)))
    ]

    @pl.when(jnp.logical_not(last))
    def _():
        for copy in halos:
            copy.start()

    eye_h = iota((heads, heads), 0) == iota((heads, heads), 1)

    def column(row):
        return jnp.broadcast_to(
            jnp.sum(jnp.where(eye_h, row, 0.0), axis=1, keepdims=True), (heads, 128)
        )

    acol[...] = column(jnp.exp(alog_ref[...]))
    skcol[...] = column(skip_ref[...])
    steps_all = jnp.log1p(jnp.exp(dt_ref[...]))
    step_row[...] = steps_all
    upto = (iota((tok, tok), 0) <= iota((tok, tok), 1)).astype(F32)
    cum_row[...] = exact(-acol[...] * steps_all, upto)

    @pl.when(first)
    def _():
        halo_x[...] = jnp.zeros_like(halo_x)
        halo_b[...] = jnp.zeros_like(halo_b)
        halo_c[...] = jnp.zeros_like(halo_c)

    @pl.when(jnp.logical_not(first))
    def _():
        for copy in halos:
            copy.wait_recv()

    spread = (iota((per, gw), 1) // hd == iota((per, gw), 0)).astype(F32)
    spread_b = spread.astype(BF16)
    lane_of = iota((tok, bw), 1) // hd
    lower = iota((tok, tok), 0) >= iota((tok, tok), 1)
    upper = iota((tok, tok), 0) <= iota((tok, tok), 1)

    def conv(src, halo, w_ref, at, width):
        cols = pl.ds(at, width)
        ext[0:8, :width] = halo[:, cols].astype(F32)[8:16]
        ext[8 : 8 + tok, :width] = src[:, cols].astype(F32)
        w = w_ref[:, cols]
        total = w[0:1] * ext[9 - taps : 9 - taps + tok, :width]
        for k in range(1, taps):
            total = total + w[k : k + 1] * ext[9 - taps + k : 9 - taps + k + tok, :width]
        return total

    def local(g, _):
        at, nat, hat = (pl.multiple_of(g * w, w) for w in (gw, nn, per))
        cols, ncols, rows = pl.ds(at, gw), pl.ds(nat, nn), pl.ds(hat, per)
        px = conv(x_ref, halo_x, wx_ref, at, gw)
        pre_x[:, cols] = px
        s = px * sigmoid(px)
        sig[:, cols] = s
        pb = conv(b_ref, halo_b, wb_ref, nat, nn)
        pre_b[:, ncols] = pb
        bv = pb * sigmoid(pb)
        bco[:, ncols] = bv
        pc = conv(c_ref, halo_c, wc_ref, nat, nn)
        pre_c[:, ncols] = pc
        cco[:, ncols] = pc * sigmoid(pc)
        cum, st = cum_row[rows, :], step_row[rows, :]
        cl = cum[:, tok - 1 : tok]
        cum_t[g] = jnp.concatenate([cum, jnp.zeros((128 - per, tok), F32)], axis=0).T
        sx = exact(st, spread, TN)
        step_x[:, cols] = sx
        ecum_x[:, cols] = exact(jnp.exp(cum), spread, TN)
        ex = exact(jnp.exp(cl - cum), spread, TN)
        e_x[:, cols] = ex
        hrows = pl.ds(at, gw)
        dec_x[hrows, :] = exact(spread, jnp.broadcast_to(jnp.exp(cl), (per, nn)), TN)
        summ[hrows, :] = dot3(split(s * sx * ex), split(bv), TN)
        return 0

    lax.fori_loop(0, groups, local, 0)

    @pl.when(first)
    def _():
        ent[...] = state_ref[...]

    def piece(k):
        return pl.ds(pl.multiple_of(k * bw, bw), bw)

    def forward_copy(k):
        return remote(exi.at[piece(k), :], ent.at[piece(k), :], fs_sem.at[k], fr_sem.at[k], after)

    def forward(k, _):
        @pl.when(jnp.logical_not(first))
        def _():
            forward_copy(k).wait_recv()

        rows = piece(k)
        exi[rows, :] = dec_x[rows, :] * ent[rows, :] + summ[rows, :]

        @pl.when(jnp.logical_not(last))
        def _():
            forward_copy(k).start()

        return 0

    lax.fori_loop(0, chunks, forward, 0)

    def backward_copy(k):
        return remote(back.at[piece(k), :], d_exi.at[piece(k), :], bs_sem.at[k], br_sem.at[k], before)

    def backward(k, _):
        @pl.when(jnp.logical_not(last))
        def _():
            backward_copy(k).wait_recv()

        @pl.when(jnp.logical_not(first))
        def _():
            rows = piece(k)
            back[rows, :] = dec_x[rows, :] * d_exi[rows, :] + d_ent[rows, :]
            backward_copy(k).start()

        return 0

    @pl.when(last)
    def _():
        d_exi[...] = jnp.zeros_like(d_exi)

    def output(g, _):
        at, nat, hat = (pl.multiple_of(g * w, w) for w in (gw, nn, per))
        cols, ncols, rows = pl.ds(at, gw), pl.ds(nat, nn), pl.ds(hat, per)
        bs, cs = split(bco[:, ncols]), split(cco[:, ncols])
        scores = dot3(cs, bs, NT)
        scores_t = dot3(bs, cs, NT)
        ents = split(ent[pl.ds(at, gw), :])
        s = sig[:, cols]
        sc = step_x[:, cols] * s
        cum, cum_c = cum_row[rows, :], cum_t[g]
        within = []
        for j in range(blocks):
            sc4 = sc[:, j * bw : (j + 1) * bw]
            ms, rs = [], []
            for i in range(BLOCK):
                h = j * BLOCK + i
                gap = cum_c[:, h : h + 1] - cum[h : h + 1, :]
                mask = jnp.exp(jnp.where(lower, gap, -1e30))
                mask_s[h] = mask
                ms.append(split(scores * mask))
                rs.append(split(jnp.where(lane_of == i, sc4, 0.0)))
            m = tuple(jnp.concatenate([v[q] for v in ms], axis=1) for q in (0, 1))
            r = tuple(jnp.concatenate([v[q] for v in rs], axis=0) for q in (0, 1))
            within.append(dot3(m, r, NN))
        inner = jnp.concatenate(within, axis=1) + ecum_x[:, cols] * dot3(cs, ents, NT)
        skx = jnp.sum(spread * skcol[rows, 0:1], axis=0, keepdims=True)
        mixed = inner + skx * s
        z = z_ref[:, cols].astype(F32)
        zs = sigmoid(z)
        sz = z * zs
        gated = mixed * sz
        inv = lax.rsqrt(jnp.mean(gated * gated, axis=1, keepdims=True) + EPS)
        dn = go_ref[:, cols].astype(F32) * gain_ref[:, cols]
        unit = gated * inv
        dg = inv * (dn - unit * jnp.mean(dn * unit, axis=1, keepdims=True))
        gz_ref[:, cols] = (dg * mixed * (zs + sz * (1.0 - zs))).astype(BF16)
        dm = dg * sz
        dm_s[:, cols] = dm
        r1_s[rows, :] = sum(dot(spread_b, v, NT) for v in split(dm * inner))
        dcar = split(dm * ecum_x[:, cols])
        d_ent[pl.ds(at, gw), :] = dot3(dcar, cs, TN)

        @pl.when(last)
        def _():
            lax.fori_loop(g * blocks, (g + 1) * blocks, backward, 0)

        ds = jnp.zeros((tok, tok), F32)
        for j in range(blocks):
            dm4 = dm[:, j * bw : (j + 1) * bw]
            scs = split(sc[:, j * bw : (j + 1) * bw])
            ms, rs = [], []
            for i in range(BLOCK):
                h = j * BLOCK + i
                gap = cum[h : h + 1, :] - cum_c[:, h : h + 1]
                ms.append(split(scores_t * jnp.exp(jnp.where(upper, gap, -1e30))))
                rs.append(split(jnp.where(lane_of == i, dm4, 0.0)))
                ds = ds + dot3(rs[-1], scs, NT) * mask_s[h]
            m = tuple(jnp.concatenate([v[q] for v in ms], axis=1) for q in (0, 1))
            r = tuple(jnp.concatenate([v[q] for v in rs], axis=0) for q in (0, 1))
            dsc_s[:, pl.ds(at + j * bw, bw)] = dot3(m, r, NN)
        dss = split(ds)
        dcs[:, ncols] = dot3(dss, bs, NN) + dot3(dcar, ents, NN)
        dbs[:, ncols] = dot3(dss, cs, TN)
        return 0

    lax.fori_loop(0, groups, output, 0)

    from_t = (iota((tok, tok), 0) >= iota((tok, tok), 1)).astype(F32)

    def grad_copy(g):
        return remote(gsend.at[g], ghalo.at[g], gs_sem.at[g], gr_sem.at[g], before)

    def silu_back(grad, pre):
        s = sigmoid(pre)
        return grad * (s + pre * s * (1.0 - s))

    def closing(g, _):
        at, nat, hat = (pl.multiple_of(g * w, w) for w in (gw, nn, per))
        cols, ncols, rows = pl.ds(at, gw), pl.ds(nat, nn), pl.ds(hat, per)

        @pl.when(jnp.logical_not(last))
        def _():
            lax.fori_loop(g * blocks, (g + 1) * blocks, backward, 0)

        grad = d_exi[pl.ds(at, gw), :]
        grads = split(grad)
        s, sx, ex = sig[:, cols], step_x[:, cols], e_x[:, cols]
        bs = split(bco[:, ncols])
        both = dsc_s[:, cols] + ex * dot3(bs, grads, NT)
        skx = jnp.sum(spread * skcol[rows, 0:1], axis=0, keepdims=True)
        gpx = silu_back(sx * both + skx * dm_s[:, cols], pre_x[:, cols])
        db = dbs[:, ncols] + dot3(split(s * sx * ex), grads, NN)
        gpbv = silu_back(db, pre_b[:, ncols])
        gpcv = silu_back(dcs[:, ncols], pre_c[:, ncols])
        gp[0:tok, cols] = gpx
        gpb[g, 0:tok, 0:nn] = gpbv
        gpb[g, 0:tok, nn : 2 * nn] = gpcv

        @pl.when(jnp.logical_not(first))
        def _():
            gsend[g, :, 0:gw] = gpx[0:8]
            gsend[g, :, gw : gw + nn] = gpbv[0:8]
            gsend[g, :, gw + nn :] = gpcv[0:8]
            grad_copy(g).start()

        u = sum(dot(spread_b, v, NT) for v in split(s * both))
        lane = jnp.sum(exact(spread, grad * exi[pl.ds(at, gw), :]), axis=1, keepdims=True)
        st = step_row[rows, :]
        d_rate = exact(r1_s[rows, :] - st * u, from_t) + lane
        gdt_ref[rows, :] = (u - acol[rows, :] * d_rate) * sigmoid(dt_ref[rows, :])
        return 0

    lax.fori_loop(0, groups, closing, 0)

    @pl.when(last)
    def _():
        ghalo[...] = jnp.zeros_like(ghalo)

    def finish(g, _):
        at, nat = (pl.multiple_of(g * w, w) for w in (gw, nn))
        cols, ncols = pl.ds(at, gw), pl.ds(nat, nn)

        @pl.when(jnp.logical_not(last))
        def _():
            grad_copy(g).wait_recv()

        gp[tok : tok + 8, cols] = ghalo[g, :, 0:gw]
        gpb[g, tok : tok + 8, :] = ghalo[g, :, gw:]
        tx = tb = tc = 0.0
        for k in range(taps):
            row = slice(taps - 1 - k, taps - 1 - k + tok)
            tx = tx + wx_ref[k : k + 1, cols] * gp[row, cols]
            tb = tb + wb_ref[k : k + 1, ncols] * gpb[g, row, 0:nn]
            tc = tc + wc_ref[k : k + 1, ncols] * gpb[g, row, nn : 2 * nn]
        gx_ref[:, cols] = tx.astype(BF16)
        gb_ref[:, ncols] = tb.astype(BF16)
        gc_ref[:, ncols] = tc.astype(BF16)
        return 0

    lax.fori_loop(0, groups, finish, 0)

    @pl.when(jnp.logical_not(last))
    def _():
        for copy in halos:
            copy.wait_send()

        def drain(k, _):
            forward_copy(k).wait_send()
            return 0

        lax.fori_loop(0, chunks, drain, 0)

    @pl.when(jnp.logical_not(first))
    def _():
        def drain(k, _):
            backward_copy(k).wait_send()
            return 0

        lax.fori_loop(0, chunks, drain, 0)

        def drain_halo(g, _):
            grad_copy(g).wait_send()
            return 0

        lax.fori_loop(0, groups, drain_halo, 0)


def per_device(
    x_stream, z_stream, b_stream, c_stream, dt_raw, a_log, skip_coef, conv_x, conv_b, conv_c, norm_gain, state_in, grad_out
):
    tok, chan = x_stream.shape
    heads, hd, nn = state_in.shape
    wide = b_stream.shape[1]
    groups = wide // nn
    per, gw = heads // groups, chan // groups
    chunks = chan // (BLOCK * hd)
    dma = pltpu.SemaphoreType.DMA

    def v(*shape, dtype=F32):
        return pltpu.VMEM(shape, dtype)

    scratch = [
        v(16, chan, dtype=BF16), v(16, wide, dtype=BF16), v(16, wide, dtype=BF16),
        v(tok + 8, gw), v(tok, chan), v(tok, wide), v(tok, wide), v(tok, chan), v(tok, wide), v(tok, wide),
        v(heads, tok), v(heads, tok), v(heads, 128), v(heads, 128), v(groups, tok, 128),
        v(tok, chan), v(tok, chan), v(tok, chan), v(chan, nn),
        v(chan, nn), v(chan, nn), v(chan, nn), v(chan, nn), v(chan, nn), v(chan, nn),
        v(tok, chan), v(heads, tok), v(tok, chan), v(tok, wide), v(tok, wide), v(per, tok, tok),
        v(tok + 8, chan), v(groups, 8, gw + 2 * nn), v(groups, 8, gw + 2 * nn), v(groups, tok + 8, 2 * nn),
        dma((3,)), dma((3,)), dma((chunks,)), dma((chunks,)), dma((chunks,)), dma((chunks,)),
        dma((groups,)), dma((groups,)),
    ]
    vmem = pl.BlockSpec(memory_space=pltpu.VMEM)
    outs = [
        jax.ShapeDtypeStruct(a.shape, a.dtype) for a in (x_stream, z_stream, b_stream, c_stream, dt_raw)
    ]
    return pl.pallas_call(
        kernel,
        out_shape=outs,
        in_specs=[vmem] * 13,
        out_specs=[vmem] * 5,
        scratch_shapes=scratch,
        compiler_params=pltpu.CompilerParams(
            collective_id=0, has_side_effects=True, vmem_limit_bytes=56 * 2**20
        ),
    )(
        x_stream, z_stream, b_stream, c_stream, dt_raw, a_log.reshape(1, heads), skip_coef.reshape(1, heads),
        conv_x, conv_b, conv_c, norm_gain.reshape(1, chan), state_in.reshape(heads * hd, nn), grad_out,
    )


def solution(mesh):
    rows = P(("group", "seq"), "head")
    turned = P("head", ("group", "seq"))
    taps = P(None, "head")
    return jax.shard_map(
        per_device,
        mesh=mesh,
        in_specs=(
            rows, rows, rows, rows, turned, P(("group", "head")), P("head"), taps, taps, taps, P("head"),
            P(("group", "head"), None, None), rows,
        ),
        out_specs=(rows, rows, rows, rows, turned),
        check_vma=False,
    )
```

```python
import functools

import jax
import jax.numpy as jnp
from jax import lax
from jax.experimental import pallas as pl
from jax.experimental.pallas import tpu as pltpu
from jax.sharding import PartitionSpec as P

EPS = 1e-05
EXACT = lax.Precision.HIGHEST
MESH = pl.DeviceIdType.MESH
F32, BF16 = jnp.float32, jnp.bfloat16
NN, NT, TN = (((1,), (0,)), ((1,), (1,)), ((0,), (0,)))
BLOCK = 4


def split(a):
    high = a.astype(BF16)
    return high, (a - high.astype(F32)).astype(BF16)


def dot(a, b, dims):
    return lax.dot_general(a, b, (dims, ((), ())), preferred_element_type=F32)


def dot3(a, b, dims):
    (ah, al), (bh, bl) = a, b
    return dot(ah, bh, dims) + (dot(ah, bl, dims) + dot(al, bh, dims))


def exact(a, b, dims=NN):
    return lax.dot_general(a, b, (dims, ((), ())), precision=EXACT, preferred_element_type=F32)


def iota(shape, dim):
    return lax.broadcasted_iota(jnp.int32, shape, dim)


def sigmoid(v):
    return 1.0 / (1.0 + jnp.exp(-v))


def kernel(
    x_ref, z_ref, b_ref, c_ref, dt_ref, alog_ref, skip_ref, wx_ref, wb_ref, wc_ref, gain_ref, state_ref, go_ref,
    gx_ref, gz_ref, gb_ref, gc_ref, gdt_ref,
    halo_x, halo_b, halo_c, ext, pre_x, pre_b, pre_c, sig, bco, cco, step_row, cum_row, acol, skcol, cum_t,
    step_x, ecum_x, e_x, dec_x, pdec_x, decs, pdecs,
    summ, psum, ebuf, ent, f_out, f_other, d_ent, pd_ent, gbuf, d_exi, b_out, b_other, dm_s, r1_s, dsc_s, dbs, dcs, mask_s,
    gp, ghalo, gsend, gpb,
    hs_sem, hr_sem, chunk_sem, gs_sem, gr_sem,
):
    me, peers = lax.axis_index("seq"), lax.axis_size("seq")
    first, last = me == 0, me == peers - 1
    tok, chan = x_ref.shape
    heads = dt_ref.shape[0]
    hd = chan // heads
    nn = state_ref.shape[1]
    groups = b_ref.shape[1] // nn
    per = heads // groups
    gw = chan // groups
    bw = BLOCK * hd
    blocks = gw // bw
    taps = wx_ref.shape[0]
    half = blocks // 2
    own = groups * half
    side, pair, pairs = lax.rem(me, 2), me // 2, peers // 2
    first_pair, last_pair = pair == 0, pair == pairs - 1
    left = side == 0
    partner = {"seq": me + 1 - 2 * side}
    pair_before, pair_after = {"seq": jnp.maximum(me - 2, 0)}, {"seq": jnp.minimum(me + 2, peers - 1)}
    before, after = {"seq": jnp.maximum(me - 1, 0)}, {"seq": jnp.minimum(me + 1, peers - 1)}

    barrier = pltpu.get_barrier_semaphore()

    for there, to in ((first, before), (last, after), (first_pair, pair_before), (last_pair, pair_after)):

        @pl.when(jnp.logical_not(there))
        def _(to=to):
            pl.semaphore_signal(barrier, inc=1, device_id=to, device_id_type=MESH)

    ahead = peers - 1 - me
    pl.semaphore_wait(
        barrier,
        jnp.minimum(me, 1) + jnp.minimum(me // 2, 1) + jnp.minimum(ahead, 1) + jnp.minimum(ahead // 2, 1),
    )

    def remote(src, dst, ssem, rsem, to):
        return pltpu.make_async_remote_copy(
            src_ref=src, dst_ref=dst, send_sem=ssem, recv_sem=rsem, device_id=to, device_id_type=MESH
        )

    halos = [
        remote(src.at[pl.ds(tok - 16, 16), :], dst, hs_sem.at[i], hr_sem.at[i], after)
        for i, (src, dst) in enumerate(((x_ref, halo_x), (b_ref, halo_b), (c_ref, halo_c)))
    ]

    @pl.when(jnp.logical_not(last))
    def _():
        for copy in halos:
            copy.start()

    eye_h = iota((heads, heads), 0) == iota((heads, heads), 1)

    def column(row):
        return jnp.broadcast_to(
            jnp.sum(jnp.where(eye_h, row, 0.0), axis=1, keepdims=True), (heads, 128)
        )

    acol[...] = column(jnp.exp(alog_ref[...]))
    skcol[...] = column(skip_ref[...])
    steps_all = jnp.log1p(jnp.exp(dt_ref[...]))
    step_row[...] = steps_all
    upto = (iota((tok, tok), 0) <= iota((tok, tok), 1)).astype(F32)
    cum_all = exact(-acol[...] * steps_all, upto)
    cum_row[...] = cum_all
    decs[...] = jnp.broadcast_to(jnp.exp(cum_all[:, tok - 1 : tok]), (heads, 128))
    dec_copy = remote(decs, pdecs, hs_sem.at[3], hr_sem.at[3], partner)
    dec_copy.start()

    @pl.when(first)
    def _():
        halo_x[...] = jnp.zeros_like(halo_x)
        halo_b[...] = jnp.zeros_like(halo_b)
        halo_c[...] = jnp.zeros_like(halo_c)

    @pl.when(jnp.logical_not(first))
    def _():
        for copy in halos:
            copy.wait_recv()

    spread = (iota((per, gw), 1) // hd == iota((per, gw), 0)).astype(F32)
    spread_b = spread.astype(BF16)
    lane_of = iota((tok, bw), 1) // hd
    lower = iota((tok, tok), 0) >= iota((tok, tok), 1)
    upper = iota((tok, tok), 0) <= iota((tok, tok), 1)

    def conv(src, halo, w_ref, at, width):
        cols = pl.ds(at, width)
        ext[0:8, :width] = halo[:, cols].astype(F32)[8:16]
        ext[8 : 8 + tok, :width] = src[:, cols].astype(F32)
        w = w_ref[:, cols]
        total = w[0:1] * ext[9 - taps : 9 - taps + tok, :width]
        for k in range(1, taps):
            total = total + w[k : k + 1] * ext[9 - taps + k : 9 - taps + k + tok, :width]
        return total

    def piece(k):
        return pl.ds(pl.multiple_of(k * bw, bw), bw)

    def moved(way, src, dst, k, to):
        return remote(
            src.at[piece(k), :], dst.at[piece(k), :], chunk_sem.at[way, 0, k], chunk_sem.at[way, 1, k], to
        )

    def mine(m):
        return m // half * blocks + side * half + lax.rem(m, half)

    def theirs(m):
        return m // half * blocks + (1 - side) * half + lax.rem(m, half)

    def summary_copy(k):
        return moved(0, summ, psum, k, partner)

    def forward_copy(k):
        return moved(1, f_out, ebuf, k, pair_after)

    def enter_copy(k):
        return moved(2, f_other, ent, k, partner)

    def grad_out_copy(k):
        return moved(3, d_ent, pd_ent, k, partner)

    def backward_copy(k):
        return moved(4, b_out, gbuf, k, pair_before)

    def exit_copy(k):
        return moved(5, b_other, d_exi, k, partner)

    def local(g, _):
        at, nat, hat = (pl.multiple_of(g * w, w) for w in (gw, nn, per))
        cols, ncols, rows = pl.ds(at, gw), pl.ds(nat, nn), pl.ds(hat, per)
        px = conv(x_ref, halo_x, wx_ref, at, gw)
        pre_x[:, cols] = px
        s = px * sigmoid(px)
        sig[:, cols] = s
        pb = conv(b_ref, halo_b, wb_ref, nat, nn)
        pre_b[:, ncols] = pb
        bv = pb * sigmoid(pb)
        bco[:, ncols] = bv
        pc = conv(c_ref, halo_c, wc_ref, nat, nn)
        pre_c[:, ncols] = pc
        cco[:, ncols] = pc * sigmoid(pc)
        cum, st = cum_row[rows, :], step_row[rows, :]
        cl = cum[:, tok - 1 : tok]
        cum_t[g] = jnp.concatenate([cum, jnp.zeros((128 - per, tok), F32)], axis=0).T
        sx = exact(st, spread, TN)
        step_x[:, cols] = sx
        ecum_x[:, cols] = exact(jnp.exp(cum), spread, TN)
        ex = exact(jnp.exp(cl - cum), spread, TN)
        e_x[:, cols] = ex
        hrows = pl.ds(at, gw)
        dec_x[hrows, :] = exact(spread, decs[rows, :], TN)
        summ[hrows, :] = dot3(split(s * sx * ex), split(bv), TN)
        for i in range(half):
            summary_copy(theirs(g * half + i)).start()
        return 0

    lax.fori_loop(0, groups, local, 0)

    dec_copy.wait_recv()

    def spread_decay(g, _):
        rows = pl.ds(pl.multiple_of(g * per, per), per)
        pdec_x[pl.ds(pl.multiple_of(g * gw, gw), gw), :] = exact(spread, pdecs[rows, :], TN)
        return 0

    lax.fori_loop(0, groups, spread_decay, 0)

    @pl.when(first_pair)
    def _():
        ebuf[...] = state_ref[...]

    @pl.when(last_pair)
    def _():
        gbuf[...] = jnp.zeros_like(gbuf)

    def ordered(here, there):
        return jnp.where(left, here, there), jnp.where(left, there, here)

    def forward(m, _):
        k = mine(m)
        rows = piece(k)
        summary_copy(k).wait_recv()

        @pl.when(jnp.logical_not(first_pair))
        def _():
            forward_copy(k).wait_recv()

        decay_a, decay_b = ordered(dec_x[rows, :], pdec_x[rows, :])
        sum_a, sum_b = ordered(summ[rows, :], psum[rows, :])
        enter = ebuf[rows, :]
        middle = decay_a * enter + sum_a

        @pl.when(jnp.logical_not(last_pair))
        def _():
            f_out[rows, :] = decay_b * middle + sum_b
            forward_copy(k).start()

        ent[rows, :], f_other[rows, :] = ordered(enter, middle)
        enter_copy(k).start()
        return 0

    def backward(m, _):
        k = mine(m)
        rows = piece(k)
        grad_out_copy(k).wait_recv()

        @pl.when(jnp.logical_not(last_pair))
        def _():
            backward_copy(k).wait_recv()

        decay_a, decay_b = ordered(dec_x[rows, :], pdec_x[rows, :])
        grad_a, grad_b = ordered(d_ent[rows, :], pd_ent[rows, :])
        leave = gbuf[rows, :]
        middle = decay_b * leave + grad_b

        @pl.when(jnp.logical_not(first_pair))
        def _():
            b_out[rows, :] = decay_a * middle + grad_a
            backward_copy(k).start()

        d_exi[rows, :], b_other[rows, :] = ordered(middle, leave)
        exit_copy(k).start()
        return 0

    lax.fori_loop(0, jnp.where(last_pair, half, own), forward, 0)

    def output(g, _):
        at, nat, hat = (pl.multiple_of(g * w, w) for w in (gw, nn, per))
        cols, ncols, rows = pl.ds(at, gw), pl.ds(nat, nn), pl.ds(hat, per)

        @pl.when(last_pair & (g < groups - 1))
        def _():
            lax.fori_loop((g + 1) * half, (g + 2) * half, forward, 0)

        for i in range(half):
            enter_copy(theirs(g * half + i)).wait_recv()
        bs, cs = split(bco[:, ncols]), split(cco[:, ncols])
        scores = dot3(cs, bs, NT)
        scores_t = dot3(bs, cs, NT)
        ents = split(ent[pl.ds(at, gw), :])
        s = sig[:, cols]
        sc = step_x[:, cols] * s
        cum, cum_c = cum_row[rows, :], cum_t[g]
        within = []
        for j in range(blocks):
            sc4 = sc[:, j * bw : (j + 1) * bw]
            ms, rs = [], []
            for i in range(BLOCK):
                h = j * BLOCK + i
                gap = cum_c[:, h : h + 1] - cum[h : h + 1, :]
                mask = jnp.exp(jnp.where(lower, gap, -1e30))
                mask_s[h] = mask
                ms.append(split(scores * mask))
                rs.append(split(jnp.where(lane_of == i, sc4, 0.0)))
            m = tuple(jnp.concatenate([v[q] for v in ms], axis=1) for q in (0, 1))
            r = tuple(jnp.concatenate([v[q] for v in rs], axis=0) for q in (0, 1))
            within.append(dot3(m, r, NN))
        inner = jnp.concatenate(within, axis=1) + ecum_x[:, cols] * dot3(cs, ents, NT)
        skx = jnp.sum(spread * skcol[rows, 0:1], axis=0, keepdims=True)
        mixed = inner + skx * s
        z = z_ref[:, cols].astype(F32)
        zs = sigmoid(z)
        sz = z * zs
        gated = mixed * sz
        inv = lax.rsqrt(jnp.mean(gated * gated, axis=1, keepdims=True) + EPS)
        dn = go_ref[:, cols].astype(F32) * gain_ref[:, cols]
        unit = gated * inv
        dg = inv * (dn - unit * jnp.mean(dn * unit, axis=1, keepdims=True))
        gz_ref[:, cols] = (dg * mixed * (zs + sz * (1.0 - zs))).astype(BF16)
        dm = dg * sz
        dm_s[:, cols] = dm
        r1_s[rows, :] = sum(dot(spread_b, v, NT) for v in split(dm * inner))
        dcar = split(dm * ecum_x[:, cols])
        d_ent[pl.ds(at, gw), :] = dot3(dcar, cs, TN)
        for i in range(half):
            grad_out_copy(theirs(g * half + i)).start()

        @pl.when(last_pair & (g > 0))
        def _():
            lax.fori_loop((g - 1) * half, g * half, backward, 0)

        ds = jnp.zeros((tok, tok), F32)
        for j in range(blocks):
            dm4 = dm[:, j * bw : (j + 1) * bw]
            scs = split(sc[:, j * bw : (j + 1) * bw])
            ms, rs = [], []
            for i in range(BLOCK):
                h = j * BLOCK + i
                gap = cum[h : h + 1, :] - cum_c[:, h : h + 1]
                ms.append(split(scores_t * jnp.exp(jnp.where(upper, gap, -1e30))))
                rs.append(split(jnp.where(lane_of == i, dm4, 0.0)))
                ds = ds + dot3(rs[-1], scs, NT) * mask_s[h]
            m = tuple(jnp.concatenate([v[q] for v in ms], axis=1) for q in (0, 1))
            r = tuple(jnp.concatenate([v[q] for v in rs], axis=0) for q in (0, 1))
            dsc_s[:, pl.ds(at + j * bw, bw)] = dot3(m, r, NN)
        dss = split(ds)
        dcs[:, ncols] = dot3(dss, bs, NN) + dot3(dcar, ents, NN)
        dbs[:, ncols] = dot3(dss, cs, TN)
        return 0

    lax.fori_loop(0, groups, output, 0)

    lax.fori_loop(
        jnp.where(last_pair, own - half, 0), jnp.where(first_pair, half, own), backward, 0
    )
    from_t = (iota((tok, tok), 0) >= iota((tok, tok), 1)).astype(F32)

    def grad_copy(g):
        return remote(gsend.at[g], ghalo.at[g], gs_sem.at[g], gr_sem.at[g], before)

    def silu_back(grad, pre):
        s = sigmoid(pre)
        return grad * (s + pre * s * (1.0 - s))

    def closing(g, _):
        at, nat, hat = (pl.multiple_of(g * w, w) for w in (gw, nn, per))
        cols, ncols, rows = pl.ds(at, gw), pl.ds(nat, nn), pl.ds(hat, per)

        @pl.when(first_pair & (g < groups - 1))
        def _():
            lax.fori_loop((g + 1) * half, (g + 2) * half, backward, 0)

        for i in range(half):
            exit_copy(theirs(g * half + i)).wait_recv()

        grad = d_exi[pl.ds(at, gw), :]
        grads = split(grad)
        s, sx, ex = sig[:, cols], step_x[:, cols], e_x[:, cols]
        bs = split(bco[:, ncols])
        both = dsc_s[:, cols] + ex * dot3(bs, grads, NT)
        skx = jnp.sum(spread * skcol[rows, 0:1], axis=0, keepdims=True)
        gpx = silu_back(sx * both + skx * dm_s[:, cols], pre_x[:, cols])
        db = dbs[:, ncols] + dot3(split(s * sx * ex), grads, NN)
        gpbv = silu_back(db, pre_b[:, ncols])
        gpcv = silu_back(dcs[:, ncols], pre_c[:, ncols])
        gp[0:tok, cols] = gpx
        gpb[g, 0:tok, 0:nn] = gpbv
        gpb[g, 0:tok, nn : 2 * nn] = gpcv

        @pl.when(jnp.logical_not(first))
        def _():
            gsend[g, :, 0:gw] = gpx[0:8]
            gsend[g, :, gw : gw + nn] = gpbv[0:8]
            gsend[g, :, gw + nn :] = gpcv[0:8]
            grad_copy(g).start()

        u = sum(dot(spread_b, v, NT) for v in split(s * both))
        hrows = pl.ds(at, gw)
        leave = dec_x[hrows, :] * ent[hrows, :] + summ[hrows, :]
        lane = jnp.sum(exact(spread, grad * leave), axis=1, keepdims=True)
        st = step_row[rows, :]
        d_rate = exact(r1_s[rows, :] - st * u, from_t) + lane
        gdt_ref[rows, :] = (u - acol[rows, :] * d_rate) * sigmoid(dt_ref[rows, :])
        return 0

    lax.fori_loop(0, groups, closing, 0)

    @pl.when(last)
    def _():
        ghalo[...] = jnp.zeros_like(ghalo)

    def finish(g, _):
        at, nat = (pl.multiple_of(g * w, w) for w in (gw, nn))
        cols, ncols = pl.ds(at, gw), pl.ds(nat, nn)

        @pl.when(jnp.logical_not(last))
        def _():
            grad_copy(g).wait_recv()

        gp[tok : tok + 8, cols] = ghalo[g, :, 0:gw]
        gpb[g, tok : tok + 8, :] = ghalo[g, :, gw:]
        tx = tb = tc = 0.0
        for k in range(taps):
            row = slice(taps - 1 - k, taps - 1 - k + tok)
            tx = tx + wx_ref[k : k + 1, cols] * gp[row, cols]
            tb = tb + wb_ref[k : k + 1, ncols] * gpb[g, row, 0:nn]
            tc = tc + wc_ref[k : k + 1, ncols] * gpb[g, row, nn : 2 * nn]
        gx_ref[:, cols] = tx.astype(BF16)
        gb_ref[:, ncols] = tb.astype(BF16)
        gc_ref[:, ncols] = tc.astype(BF16)
        return 0

    lax.fori_loop(0, groups, finish, 0)

    dec_copy.wait_send()

    def drain(m, _):
        summary_copy(theirs(m)).wait_send()
        grad_out_copy(theirs(m)).wait_send()
        enter_copy(mine(m)).wait_send()
        exit_copy(mine(m)).wait_send()

        @pl.when(jnp.logical_not(last_pair))
        def _():
            forward_copy(mine(m)).wait_send()

        @pl.when(jnp.logical_not(first_pair))
        def _():
            backward_copy(mine(m)).wait_send()

        return 0

    lax.fori_loop(0, own, drain, 0)

    @pl.when(jnp.logical_not(last))
    def _():
        for copy in halos:
            copy.wait_send()

    @pl.when(jnp.logical_not(first))
    def _():
        def drain_halo(g, _):
            grad_copy(g).wait_send()
            return 0

        lax.fori_loop(0, groups, drain_halo, 0)


def per_device(
    x_stream, z_stream, b_stream, c_stream, dt_raw, a_log, skip_coef, conv_x, conv_b, conv_c, norm_gain, state_in, grad_out
):
    tok, chan = x_stream.shape
    heads, hd, nn = state_in.shape
    wide = b_stream.shape[1]
    groups = wide // nn
    per, gw = heads // groups, chan // groups
    chunks = chan // (BLOCK * hd)
    dma = pltpu.SemaphoreType.DMA

    def v(*shape, dtype=F32):
        return pltpu.VMEM(shape, dtype)

    scratch = [
        v(16, chan, dtype=BF16), v(16, wide, dtype=BF16), v(16, wide, dtype=BF16),
        v(tok + 8, gw), v(tok, chan), v(tok, wide), v(tok, wide), v(tok, chan), v(tok, wide), v(tok, wide),
        v(heads, tok), v(heads, tok), v(heads, 128), v(heads, 128), v(groups, tok, 128),
        v(tok, chan), v(tok, chan), v(tok, chan), v(chan, nn), v(chan, nn), v(heads, 128), v(heads, 128),
        *([v(chan, nn)] * 12),
        v(tok, chan), v(heads, tok), v(tok, chan), v(tok, wide), v(tok, wide), v(per, tok, tok),
        v(tok + 8, chan), v(groups, 8, gw + 2 * nn), v(groups, 8, gw + 2 * nn), v(groups, tok + 8, 2 * nn),
        dma((4,)), dma((4,)), dma((6, 2, chunks)), dma((groups,)), dma((groups,)),
    ]
    vmem = pl.BlockSpec(memory_space=pltpu.VMEM)
    outs = [
        jax.ShapeDtypeStruct(a.shape, a.dtype) for a in (x_stream, z_stream, b_stream, c_stream, dt_raw)
    ]
    return pl.pallas_call(
        kernel,
        out_shape=outs,
        in_specs=[vmem] * 13,
        out_specs=[vmem] * 5,
        scratch_shapes=scratch,
        compiler_params=pltpu.CompilerParams(
            collective_id=0, has_side_effects=True, vmem_limit_bytes=56 * 2**20
        ),
    )(
        x_stream, z_stream, b_stream, c_stream, dt_raw, a_log.reshape(1, heads), skip_coef.reshape(1, heads),
        conv_x, conv_b, conv_c, norm_gain.reshape(1, chan), state_in.reshape(heads * hd, nn), grad_out,
    )


def solution(mesh):
    rows = P(("group", "seq"), "head")
    turned = P("head", ("group", "seq"))
    taps = P(None, "head")
    return jax.shard_map(
        per_device,
        mesh=mesh,
        in_specs=(
            rows, rows, rows, rows, turned, P(("group", "head")), P("head"), taps, taps, taps, P("head"),
            P(("group", "head"), None, None), rows,
        ),
        out_specs=(rows, rows, rows, rows, turned),
        check_vma=False,
    )
```

```python
import functools

import jax
import jax.numpy as jnp
from jax import lax
from jax.experimental import pallas as pl
from jax.experimental.pallas import tpu as pltpu
from jax.sharding import PartitionSpec as P

EPS = 1e-05
EXACT = lax.Precision.HIGHEST
MESH = pl.DeviceIdType.MESH
F32, BF16 = jnp.float32, jnp.bfloat16
NN, NT, TN = (((1,), (0,)), ((1,), (1,)), ((0,), (0,)))
BLOCK = 4
PIECE = 4


def split(a):
    high = a.astype(BF16)
    return high, (a - high.astype(F32)).astype(BF16)


def dot(a, b, dims):
    return lax.dot_general(a, b, (dims, ((), ())), preferred_element_type=F32)


def dot3(a, b, dims):
    (ah, al), (bh, bl) = a, b
    return dot(ah, bh, dims) + (dot(ah, bl, dims) + dot(al, bh, dims))


def exact(a, b, dims=NN):
    return lax.dot_general(a, b, (dims, ((), ())), precision=EXACT, preferred_element_type=F32)


def iota(shape, dim):
    return lax.broadcasted_iota(jnp.int32, shape, dim)


def sigmoid(v):
    return 1.0 / (1.0 + jnp.exp(-v))


def kernel(
    x_ref, z_ref, b_ref, c_ref, dt_ref, alog_ref, skip_ref, wx_ref, wb_ref, wc_ref, gain_ref, state_ref, go_ref,
    gx_ref, gz_ref, gb_ref, gc_ref, gdt_ref,
    halo_x, halo_b, halo_c, ext, pre_x, pre_b, pre_c, sig, bco, cco, step_row, cum_row, acol, skcol, cum_t,
    step_x, ecum_x, e_x, dec_x, pdec_x, decs, pdecs,
    summ, psum, ebuf, ent, f_out, f_other, d_ent, pd_ent, gbuf, d_exi, b_out, b_other, dm_s, r1_s, dsc_s, dbs, dcs, mask_s,
    gp, ghalo, gsend, gpb,
    hs_sem, hr_sem, chunk_sem, gs_sem, gr_sem,
):
    me, peers = lax.axis_index("seq"), lax.axis_size("seq")
    first, last = me == 0, me == peers - 1
    tok, chan = x_ref.shape
    heads = dt_ref.shape[0]
    hd = chan // heads
    nn = state_ref.shape[1]
    groups = b_ref.shape[1] // nn
    per = heads // groups
    gw = chan // groups
    bw = BLOCK * hd
    blocks = gw // bw
    taps = wx_ref.shape[0]
    cw = PIECE * hd
    pieces = gw // cw
    half = pieces // 2
    own = groups * half
    side, pair, pairs = lax.rem(me, 2), me // 2, peers // 2
    first_pair, last_pair = pair == 0, pair == pairs - 1
    left = side == 0
    partner = {"seq": me + 1 - 2 * side}
    pair_before, pair_after = {"seq": jnp.maximum(me - 2, 0)}, {"seq": jnp.minimum(me + 2, peers - 1)}
    before, after = {"seq": jnp.maximum(me - 1, 0)}, {"seq": jnp.minimum(me + 1, peers - 1)}

    barrier = pltpu.get_barrier_semaphore()

    for there, to in ((first, before), (last, after), (first_pair, pair_before), (last_pair, pair_after)):

        @pl.when(jnp.logical_not(there))
        def _(to=to):
            pl.semaphore_signal(barrier, inc=1, device_id=to, device_id_type=MESH)

    ahead = peers - 1 - me
    pl.semaphore_wait(
        barrier,
        jnp.minimum(me, 1) + jnp.minimum(me // 2, 1) + jnp.minimum(ahead, 1) + jnp.minimum(ahead // 2, 1),
    )

    def remote(src, dst, ssem, rsem, to):
        return pltpu.make_async_remote_copy(
            src_ref=src, dst_ref=dst, send_sem=ssem, recv_sem=rsem, device_id=to, device_id_type=MESH
        )

    halos = [
        remote(src.at[pl.ds(tok - 16, 16), :], dst, hs_sem.at[i], hr_sem.at[i], after)
        for i, (src, dst) in enumerate(((x_ref, halo_x), (b_ref, halo_b), (c_ref, halo_c)))
    ]

    @pl.when(jnp.logical_not(last))
    def _():
        for copy in halos:
            copy.start()

    eye_h = iota((heads, heads), 0) == iota((heads, heads), 1)

    def column(row):
        return jnp.broadcast_to(
            jnp.sum(jnp.where(eye_h, row, 0.0), axis=1, keepdims=True), (heads, 128)
        )

    acol[...] = column(jnp.exp(alog_ref[...]))
    skcol[...] = column(skip_ref[...])
    steps_all = jnp.log1p(jnp.exp(dt_ref[...]))
    step_row[...] = steps_all
    upto = (iota((tok, tok), 0) <= iota((tok, tok), 1)).astype(F32)
    cum_all = exact(-acol[...] * steps_all, upto)
    cum_row[...] = cum_all
    decs[...] = jnp.broadcast_to(jnp.exp(cum_all[:, tok - 1 : tok]), (heads, 128))
    dec_copy = remote(decs, pdecs, hs_sem.at[3], hr_sem.at[3], partner)
    dec_copy.start()

    @pl.when(first)
    def _():
        halo_x[...] = jnp.zeros_like(halo_x)
        halo_b[...] = jnp.zeros_like(halo_b)
        halo_c[...] = jnp.zeros_like(halo_c)

    @pl.when(jnp.logical_not(first))
    def _():
        for copy in halos:
            copy.wait_recv()

    spread = (iota((per, gw), 1) // hd == iota((per, gw), 0)).astype(F32)
    spread_b = spread.astype(BF16)
    lane_of = iota((tok, bw), 1) // hd
    lower = iota((tok, tok), 0) >= iota((tok, tok), 1)
    upper = iota((tok, tok), 0) <= iota((tok, tok), 1)

    def conv(src, halo, w_ref, at, width):
        cols = pl.ds(at, width)
        ext[0:8, :width] = halo[:, cols].astype(F32)[8:16]
        ext[8 : 8 + tok, :width] = src[:, cols].astype(F32)
        w = w_ref[:, cols]
        total = w[0:1] * ext[9 - taps : 9 - taps + tok, :width]
        for k in range(1, taps):
            total = total + w[k : k + 1] * ext[9 - taps + k : 9 - taps + k + tok, :width]
        return total

    def piece(k):
        return pl.ds(pl.multiple_of(k * cw, cw), cw)

    def moved(way, src, dst, k, to):
        return remote(
            src.at[piece(k), :], dst.at[piece(k), :], chunk_sem.at[way, 0, k], chunk_sem.at[way, 1, k], to
        )

    def mine(m):
        return m // half * pieces + side * half + lax.rem(m, half)

    def theirs(m):
        return m // half * pieces + (1 - side) * half + lax.rem(m, half)

    def summary_copy(k):
        return moved(0, summ, psum, k, partner)

    def forward_copy(k):
        return moved(1, f_out, ebuf, k, pair_after)

    def enter_copy(k):
        return moved(2, f_other, ent, k, partner)

    def grad_out_copy(k):
        return moved(3, d_ent, pd_ent, k, partner)

    def backward_copy(k):
        return moved(4, b_out, gbuf, k, pair_before)

    def exit_copy(k):
        return moved(5, b_other, d_exi, k, partner)

    def local(g, _):
        at, nat, hat = (pl.multiple_of(g * w, w) for w in (gw, nn, per))
        cols, ncols, rows = pl.ds(at, gw), pl.ds(nat, nn), pl.ds(hat, per)
        px = conv(x_ref, halo_x, wx_ref, at, gw)
        pre_x[:, cols] = px
        s = px * sigmoid(px)
        sig[:, cols] = s
        pb = conv(b_ref, halo_b, wb_ref, nat, nn)
        pre_b[:, ncols] = pb
        bv = pb * sigmoid(pb)
        bco[:, ncols] = bv
        pc = conv(c_ref, halo_c, wc_ref, nat, nn)
        pre_c[:, ncols] = pc
        cco[:, ncols] = pc * sigmoid(pc)
        cum, st = cum_row[rows, :], step_row[rows, :]
        cl = cum[:, tok - 1 : tok]
        cum_t[g] = jnp.concatenate([cum, jnp.zeros((128 - per, tok), F32)], axis=0).T
        sx = exact(st, spread, TN)
        step_x[:, cols] = sx
        ecum_x[:, cols] = exact(jnp.exp(cum), spread, TN)
        ex = exact(jnp.exp(cl - cum), spread, TN)
        e_x[:, cols] = ex
        hrows = pl.ds(at, gw)
        dec_x[hrows, :] = exact(spread, decs[rows, :], TN)
        summ[hrows, :] = dot3(split(s * sx * ex), split(bv), TN)
        for i in range(half):
            summary_copy(theirs(g * half + i)).start()
        return 0

    lax.fori_loop(0, groups, local, 0)

    dec_copy.wait_recv()

    def spread_decay(g, _):
        rows = pl.ds(pl.multiple_of(g * per, per), per)
        pdec_x[pl.ds(pl.multiple_of(g * gw, gw), gw), :] = exact(spread, pdecs[rows, :], TN)
        return 0

    lax.fori_loop(0, groups, spread_decay, 0)

    @pl.when(first_pair)
    def _():
        ebuf[...] = state_ref[...]

    @pl.when(last_pair)
    def _():
        gbuf[...] = jnp.zeros_like(gbuf)

    def ordered(here, there):
        return jnp.where(left, here, there), jnp.where(left, there, here)

    def forward(m, _):
        k = mine(m)
        rows = piece(k)
        summary_copy(k).wait_recv()

        @pl.when(jnp.logical_not(first_pair))
        def _():
            forward_copy(k).wait_recv()

        decay_a, decay_b = ordered(dec_x[rows, :], pdec_x[rows, :])
        sum_a, sum_b = ordered(summ[rows, :], psum[rows, :])
        enter = ebuf[rows, :]
        middle = decay_a * enter + sum_a

        @pl.when(jnp.logical_not(last_pair))
        def _():
            f_out[rows, :] = decay_b * middle + sum_b
            forward_copy(k).start()

        ent[rows, :], f_other[rows, :] = ordered(enter, middle)
        enter_copy(k).start()
        return 0

    def backward(m, _):
        k = mine(m)
        rows = piece(k)
        grad_out_copy(k).wait_recv()

        @pl.when(jnp.logical_not(last_pair))
        def _():
            backward_copy(k).wait_recv()

        decay_a, decay_b = ordered(dec_x[rows, :], pdec_x[rows, :])
        grad_a, grad_b = ordered(d_ent[rows, :], pd_ent[rows, :])
        leave = gbuf[rows, :]
        middle = decay_b * leave + grad_b

        @pl.when(jnp.logical_not(first_pair))
        def _():
            b_out[rows, :] = decay_a * middle + grad_a
            backward_copy(k).start()

        d_exi[rows, :], b_other[rows, :] = ordered(middle, leave)
        exit_copy(k).start()
        return 0

    lax.fori_loop(0, jnp.where(last_pair, half, own), forward, 0)

    def output(g, _):
        at, nat, hat = (pl.multiple_of(g * w, w) for w in (gw, nn, per))
        cols, ncols, rows = pl.ds(at, gw), pl.ds(nat, nn), pl.ds(hat, per)

        @pl.when(last_pair & (g < groups - 1))
        def _():
            lax.fori_loop((g + 1) * half, (g + 2) * half, forward, 0)

        for i in range(half):
            enter_copy(theirs(g * half + i)).wait_recv()
        bs, cs = split(bco[:, ncols]), split(cco[:, ncols])
        scores = dot3(cs, bs, NT)
        scores_t = dot3(bs, cs, NT)
        ents = split(ent[pl.ds(at, gw), :])
        s = sig[:, cols]
        sc = step_x[:, cols] * s
        cum, cum_c = cum_row[rows, :], cum_t[g]
        within = []
        for j in range(blocks):
            sc4 = sc[:, j * bw : (j + 1) * bw]
            ms, rs = [], []
            for i in range(BLOCK):
                h = j * BLOCK + i
                gap = cum_c[:, h : h + 1] - cum[h : h + 1, :]
                mask = jnp.exp(jnp.where(lower, gap, -1e30))
                mask_s[h] = mask
                ms.append(split(scores * mask))
                rs.append(split(jnp.where(lane_of == i, sc4, 0.0)))
            m = tuple(jnp.concatenate([v[q] for v in ms], axis=1) for q in (0, 1))
            r = tuple(jnp.concatenate([v[q] for v in rs], axis=0) for q in (0, 1))
            within.append(dot3(m, r, NN))
        inner = jnp.concatenate(within, axis=1) + ecum_x[:, cols] * dot3(cs, ents, NT)
        skx = jnp.sum(spread * skcol[rows, 0:1], axis=0, keepdims=True)
        mixed = inner + skx * s
        z = z_ref[:, cols].astype(F32)
        zs = sigmoid(z)
        sz = z * zs
        gated = mixed * sz
        inv = lax.rsqrt(jnp.mean(gated * gated, axis=1, keepdims=True) + EPS)
        dn = go_ref[:, cols].astype(F32) * gain_ref[:, cols]
        unit = gated * inv
        dg = inv * (dn - unit * jnp.mean(dn * unit, axis=1, keepdims=True))
        gz_ref[:, cols] = (dg * mixed * (zs + sz * (1.0 - zs))).astype(BF16)
        dm = dg * sz
        dm_s[:, cols] = dm
        r1_s[rows, :] = sum(dot(spread_b, v, NT) for v in split(dm * inner))
        dcar = split(dm * ecum_x[:, cols])
        d_ent[pl.ds(at, gw), :] = dot3(dcar, cs, TN)
        for i in range(half):
            grad_out_copy(theirs(g * half + i)).start()

        @pl.when(last_pair & (g > 0))
        def _():
            lax.fori_loop((g - 1) * half, g * half, backward, 0)

        ds = jnp.zeros((tok, tok), F32)
        for j in range(blocks):
            dm4 = dm[:, j * bw : (j + 1) * bw]
            scs = split(sc[:, j * bw : (j + 1) * bw])
            ms, rs = [], []
            for i in range(BLOCK):
                h = j * BLOCK + i
                gap = cum[h : h + 1, :] - cum_c[:, h : h + 1]
                ms.append(split(scores_t * jnp.exp(jnp.where(upper, gap, -1e30))))
                rs.append(split(jnp.where(lane_of == i, dm4, 0.0)))
                ds = ds + dot3(rs[-1], scs, NT) * mask_s[h]
            m = tuple(jnp.concatenate([v[q] for v in ms], axis=1) for q in (0, 1))
            r = tuple(jnp.concatenate([v[q] for v in rs], axis=0) for q in (0, 1))
            dsc_s[:, pl.ds(at + j * bw, bw)] = dot3(m, r, NN)
        dss = split(ds)
        dcs[:, ncols] = dot3(dss, bs, NN) + dot3(dcar, ents, NN)
        dbs[:, ncols] = dot3(dss, cs, TN)
        return 0

    lax.fori_loop(0, groups, output, 0)

    lax.fori_loop(
        jnp.where(last_pair, own - half, 0), jnp.where(first_pair, half, own), backward, 0
    )
    from_t = (iota((tok, tok), 0) >= iota((tok, tok), 1)).astype(F32)

    def grad_copy(g):
        return remote(gsend.at[g], ghalo.at[g], gs_sem.at[g], gr_sem.at[g], before)

    def silu_back(grad, pre):
        s = sigmoid(pre)
        return grad * (s + pre * s * (1.0 - s))

    def closing(g, _):
        at, nat, hat = (pl.multiple_of(g * w, w) for w in (gw, nn, per))
        cols, ncols, rows = pl.ds(at, gw), pl.ds(nat, nn), pl.ds(hat, per)

        @pl.when(first_pair & (g < groups - 1))
        def _():
            lax.fori_loop((g + 1) * half, (g + 2) * half, backward, 0)

        for i in range(half):
            exit_copy(theirs(g * half + i)).wait_recv()

        grad = d_exi[pl.ds(at, gw), :]
        grads = split(grad)
        s, sx, ex = sig[:, cols], step_x[:, cols], e_x[:, cols]
        bs = split(bco[:, ncols])
        both = dsc_s[:, cols] + ex * dot3(bs, grads, NT)
        skx = jnp.sum(spread * skcol[rows, 0:1], axis=0, keepdims=True)
        gpx = silu_back(sx * both + skx * dm_s[:, cols], pre_x[:, cols])
        db = dbs[:, ncols] + dot3(split(s * sx * ex), grads, NN)
        gpbv = silu_back(db, pre_b[:, ncols])
        gpcv = silu_back(dcs[:, ncols], pre_c[:, ncols])
        gp[0:tok, cols] = gpx
        gpb[g, 0:tok, 0:nn] = gpbv
        gpb[g, 0:tok, nn : 2 * nn] = gpcv

        @pl.when(jnp.logical_not(first))
        def _():
            gsend[g, :, 0:gw] = gpx[0:8]
            gsend[g, :, gw : gw + nn] = gpbv[0:8]
            gsend[g, :, gw + nn :] = gpcv[0:8]
            grad_copy(g).start()

        u = sum(dot(spread_b, v, NT) for v in split(s * both))
        hrows = pl.ds(at, gw)
        leave = dec_x[hrows, :] * ent[hrows, :] + summ[hrows, :]
        lane = jnp.sum(exact(spread, grad * leave), axis=1, keepdims=True)
        st = step_row[rows, :]
        d_rate = exact(r1_s[rows, :] - st * u, from_t) + lane
        gdt_ref[rows, :] = (u - acol[rows, :] * d_rate) * sigmoid(dt_ref[rows, :])
        return 0

    lax.fori_loop(0, groups, closing, 0)

    @pl.when(last)
    def _():
        ghalo[...] = jnp.zeros_like(ghalo)

    def finish(g, _):
        at, nat = (pl.multiple_of(g * w, w) for w in (gw, nn))
        cols, ncols = pl.ds(at, gw), pl.ds(nat, nn)

        @pl.when(jnp.logical_not(last))
        def _():
            grad_copy(g).wait_recv()

        gp[tok : tok + 8, cols] = ghalo[g, :, 0:gw]
        gpb[g, tok : tok + 8, :] = ghalo[g, :, gw:]
        tx = tb = tc = 0.0
        for k in range(taps):
            row = slice(taps - 1 - k, taps - 1 - k + tok)
            tx = tx + wx_ref[k : k + 1, cols] * gp[row, cols]
            tb = tb + wb_ref[k : k + 1, ncols] * gpb[g, row, 0:nn]
            tc = tc + wc_ref[k : k + 1, ncols] * gpb[g, row, nn : 2 * nn]
        gx_ref[:, cols] = tx.astype(BF16)
        gb_ref[:, ncols] = tb.astype(BF16)
        gc_ref[:, ncols] = tc.astype(BF16)
        return 0

    lax.fori_loop(0, groups, finish, 0)

    dec_copy.wait_send()

    def drain(m, _):
        summary_copy(theirs(m)).wait_send()
        grad_out_copy(theirs(m)).wait_send()
        enter_copy(mine(m)).wait_send()
        exit_copy(mine(m)).wait_send()

        @pl.when(jnp.logical_not(last_pair))
        def _():
            forward_copy(mine(m)).wait_send()

        @pl.when(jnp.logical_not(first_pair))
        def _():
            backward_copy(mine(m)).wait_send()

        return 0

    lax.fori_loop(0, own, drain, 0)

    @pl.when(jnp.logical_not(last))
    def _():
        for copy in halos:
            copy.wait_send()

    @pl.when(jnp.logical_not(first))
    def _():
        def drain_halo(g, _):
            grad_copy(g).wait_send()
            return 0

        lax.fori_loop(0, groups, drain_halo, 0)


def write_out(*refs):
    count = len(refs) // 2
    for src, dst in zip(refs[:count], refs[count:]):
        dst[...] = src[...]


def per_device(
    x_stream, z_stream, b_stream, c_stream, dt_raw, a_log, skip_coef, conv_x, conv_b, conv_c, norm_gain, state_in, grad_out
):
    tok, chan = x_stream.shape
    heads, hd, nn = state_in.shape
    wide = b_stream.shape[1]
    groups = wide // nn
    per, gw = heads // groups, chan // groups
    chunks = chan // (PIECE * hd)
    dma = pltpu.SemaphoreType.DMA

    def v(*shape, dtype=F32):
        return pltpu.VMEM(shape, dtype)

    scratch = [
        v(16, chan, dtype=BF16), v(16, wide, dtype=BF16), v(16, wide, dtype=BF16),
        v(tok + 8, gw), v(tok, chan), v(tok, wide), v(tok, wide), v(tok, chan), v(tok, wide), v(tok, wide),
        v(heads, tok), v(heads, tok), v(heads, 128), v(heads, 128), v(groups, tok, 128),
        v(tok, chan), v(tok, chan), v(tok, chan), v(chan, nn), v(chan, nn), v(heads, 128), v(heads, 128),
        *([v(chan, nn)] * 12),
        v(tok, chan), v(heads, tok), v(tok, chan), v(tok, wide), v(tok, wide), v(per, tok, tok),
        v(tok + 8, chan), v(groups, 8, gw + 2 * nn), v(groups, 8, gw + 2 * nn), v(groups, tok + 8, 2 * nn),
        dma((4,)), dma((4,)), dma((6, 2, chunks)), dma((groups,)), dma((groups,)),
    ]
    vmem = pl.BlockSpec(memory_space=pltpu.VMEM)
    outs = [
        jax.ShapeDtypeStruct(a.shape, a.dtype) for a in (x_stream, z_stream, b_stream, c_stream, dt_raw)
    ]
    results = pl.pallas_call(
        kernel,
        out_shape=outs,
        in_specs=[vmem] * 13,
        out_specs=[vmem] * 5,
        scratch_shapes=scratch,
        compiler_params=pltpu.CompilerParams(
            collective_id=0, has_side_effects=True, vmem_limit_bytes=56 * 2**20
        ),
    )(
        x_stream, z_stream, b_stream, c_stream, dt_raw, a_log.reshape(1, heads), skip_coef.reshape(1, heads),
        conv_x, conv_b, conv_c, norm_gain.reshape(1, chan), state_in.reshape(heads * hd, nn), grad_out,
    )
    return pl.pallas_call(write_out, out_shape=outs, in_specs=[vmem] * 5, out_specs=[vmem] * 5)(*results)


def solution(mesh):
    rows = P(("group", "seq"), "head")
    turned = P("head", ("group", "seq"))
    taps = P(None, "head")
    return jax.shard_map(
        per_device,
        mesh=mesh,
        in_specs=(
            rows, rows, rows, rows, turned, P(("group", "head")), P("head"), taps, taps, taps, P("head"),
            P(("group", "head"), None, None), rows,
        ),
        out_specs=(rows, rows, rows, rows, turned),
        check_vma=False,
    )
```

```python
import functools

import jax
import jax.numpy as jnp
from jax import lax
from jax.experimental import pallas as pl
from jax.experimental.pallas import tpu as pltpu
from jax.sharding import PartitionSpec as P

EPS = 1e-05
EXACT = lax.Precision.HIGHEST
MESH = pl.DeviceIdType.MESH
F32, BF16 = jnp.float32, jnp.bfloat16
NN, NT, TN = (((1,), (0,)), ((1,), (1,)), ((0,), (0,)))
BLOCK = 4
PIECE = 4


def split(a):
    high = a.astype(BF16)
    return high, (a - high.astype(F32)).astype(BF16)


def dot(a, b, dims):
    return lax.dot_general(a, b, (dims, ((), ())), preferred_element_type=F32)


def dot3(a, b, dims):
    (ah, al), (bh, bl) = a, b
    return dot(ah, bh, dims) + (dot(ah, bl, dims) + dot(al, bh, dims))


def exact(a, b, dims=NN):
    return lax.dot_general(a, b, (dims, ((), ())), precision=EXACT, preferred_element_type=F32)


def iota(shape, dim):
    return lax.broadcasted_iota(jnp.int32, shape, dim)


def sigmoid(v):
    return 1.0 / (1.0 + jnp.exp(-v))


def kernel(
    x_ref, z_ref, b_ref, c_ref, dt_ref, alog_ref, skip_ref, wx_ref, wb_ref, wc_ref, gain_ref, state_ref, go_ref,
    gx_ref, gz_ref, gb_ref, gc_ref, gdt_ref,
    halo_x, halo_b, halo_c, ext, pre_x, pre_b, pre_c, sig, bco, cco, step_row, cum_row, acol, skcol, cum_t,
    step_x, ecum_x, e_x, dec_x, pdec_x, decs, pdecs,
    summ, psum, ebuf, ent, f_out, f_other, d_ent, pd_ent, gbuf, d_exi, b_out, b_other, dm_s, r1_s, dsc_s, dbs, dcs, mask_s,
    gp, ghalo, gsend, gpb,
    hs_sem, hr_sem, chunk_sem, gs_sem, gr_sem,
):
    me, peers = lax.axis_index("seq"), lax.axis_size("seq")
    first, last = me == 0, me == peers - 1
    tok, chan = x_ref.shape
    heads = dt_ref.shape[0]
    hd = chan // heads
    nn = state_ref.shape[1]
    groups = b_ref.shape[1] // nn
    per = heads // groups
    gw = chan // groups
    bw = BLOCK * hd
    blocks = gw // bw
    taps = wx_ref.shape[0]
    cw = PIECE * hd
    pieces = gw // cw
    half = pieces // 2
    own = groups * half
    side, pair, pairs = lax.rem(me, 2), me // 2, peers // 2
    first_pair, last_pair = pair == 0, pair == pairs - 1
    left = side == 0
    partner = {"seq": me + 1 - 2 * side}
    pair_before, pair_after = {"seq": jnp.maximum(me - 2, 0)}, {"seq": jnp.minimum(me + 2, peers - 1)}
    before, after = {"seq": jnp.maximum(me - 1, 0)}, {"seq": jnp.minimum(me + 1, peers - 1)}

    barrier = pltpu.get_barrier_semaphore()

    for there, to in ((first, before), (last, after), (first_pair, pair_before), (last_pair, pair_after)):

        @pl.when(jnp.logical_not(there))
        def _(to=to):
            pl.semaphore_signal(barrier, inc=1, device_id=to, device_id_type=MESH)

    ahead = peers - 1 - me
    pl.semaphore_wait(
        barrier,
        jnp.minimum(me, 1) + jnp.minimum(me // 2, 1) + jnp.minimum(ahead, 1) + jnp.minimum(ahead // 2, 1),
    )

    def remote(src, dst, ssem, rsem, to):
        return pltpu.make_async_remote_copy(
            src_ref=src, dst_ref=dst, send_sem=ssem, recv_sem=rsem, device_id=to, device_id_type=MESH
        )

    halos = [
        remote(src.at[pl.ds(tok - 16, 16), :], dst, hs_sem.at[i], hr_sem.at[i], after)
        for i, (src, dst) in enumerate(((x_ref, halo_x), (b_ref, halo_b), (c_ref, halo_c)))
    ]

    @pl.when(jnp.logical_not(last))
    def _():
        for copy in halos:
            copy.start()

    eye_h = iota((heads, heads), 0) == iota((heads, heads), 1)

    def column(row):
        return jnp.broadcast_to(
            jnp.sum(jnp.where(eye_h, row, 0.0), axis=1, keepdims=True), (heads, 128)
        )

    acol[...] = column(jnp.exp(alog_ref[...]))
    skcol[...] = column(skip_ref[...])
    steps_all = jnp.log1p(jnp.exp(dt_ref[...]))
    step_row[...] = steps_all
    upto = (iota((tok, tok), 0) <= iota((tok, tok), 1)).astype(F32)
    cum_all = exact(-acol[...] * steps_all, upto)
    cum_row[...] = cum_all
    decs[...] = jnp.broadcast_to(jnp.exp(cum_all[:, tok - 1 : tok]), (heads, 128))
    dec_copy = remote(decs, pdecs, hs_sem.at[3], hr_sem.at[3], partner)
    dec_copy.start()

    @pl.when(first)
    def _():
        halo_x[...] = jnp.zeros_like(halo_x)
        halo_b[...] = jnp.zeros_like(halo_b)
        halo_c[...] = jnp.zeros_like(halo_c)

    @pl.when(jnp.logical_not(first))
    def _():
        for copy in halos:
            copy.wait_recv()

    spread = (iota((per, gw), 1) // hd == iota((per, gw), 0)).astype(F32)
    spread_b = spread.astype(BF16)
    lane_of = iota((tok, bw), 1) // hd
    lower = iota((tok, tok), 0) >= iota((tok, tok), 1)
    upper = iota((tok, tok), 0) <= iota((tok, tok), 1)

    def conv(src, halo, w_ref, at, width):
        cols = pl.ds(at, width)
        ext[0:8, :width] = halo[:, cols].astype(F32)[8:16]
        ext[8 : 8 + tok, :width] = src[:, cols].astype(F32)
        w = w_ref[:, cols]
        total = w[0:1] * ext[9 - taps : 9 - taps + tok, :width]
        for k in range(1, taps):
            total = total + w[k : k + 1] * ext[9 - taps + k : 9 - taps + k + tok, :width]
        return total

    def piece(k):
        return pl.ds(pl.multiple_of(k * cw, cw), cw)

    def moved(way, src, dst, k, to):
        return remote(
            src.at[piece(k), :], dst.at[piece(k), :], chunk_sem.at[way, 0, k], chunk_sem.at[way, 1, k], to
        )

    def mine(m):
        return m // half * pieces + side * half + lax.rem(m, half)

    def theirs(m):
        return m // half * pieces + (1 - side) * half + lax.rem(m, half)

    def summary_copy(k):
        return moved(0, summ, psum, k, partner)

    def forward_copy(k):
        return moved(1, f_out, ebuf, k, pair_after)

    def enter_copy(k):
        return moved(2, f_other, ent, k, partner)

    def grad_out_copy(k):
        return moved(3, d_ent, pd_ent, k, partner)

    def backward_copy(k):
        return moved(4, b_out, gbuf, k, pair_before)

    def exit_copy(k):
        return moved(5, b_other, d_exi, k, partner)

    def local(g, _):
        at, nat, hat = (pl.multiple_of(g * w, w) for w in (gw, nn, per))
        cols, ncols, rows = pl.ds(at, gw), pl.ds(nat, nn), pl.ds(hat, per)
        px = conv(x_ref, halo_x, wx_ref, at, gw)
        pre_x[:, cols] = px
        s = px * sigmoid(px)
        sig[:, cols] = s
        pb = conv(b_ref, halo_b, wb_ref, nat, nn)
        pre_b[:, ncols] = pb
        bv = pb * sigmoid(pb)
        bco[:, ncols] = bv
        cum, st = cum_row[rows, :], step_row[rows, :]
        cl = cum[:, tok - 1 : tok]
        cum_t[g] = jnp.concatenate([cum, jnp.zeros((128 - per, tok), F32)], axis=0).T
        sx = exact(st, spread, TN)
        step_x[:, cols] = sx
        ex = exact(jnp.exp(cl - cum), spread, TN)
        e_x[:, cols] = ex
        hrows = pl.ds(at, gw)
        dec_x[hrows, :] = exact(spread, decs[rows, :], TN)
        summ[hrows, :] = dot3(split(s * sx * ex), split(bv), TN)
        for i in range(half):
            summary_copy(theirs(g * half + i)).start()
        pc = conv(c_ref, halo_c, wc_ref, nat, nn)
        pre_c[:, ncols] = pc
        cco[:, ncols] = pc * sigmoid(pc)
        ecum_x[:, cols] = exact(jnp.exp(cum), spread, TN)
        return 0

    lax.fori_loop(0, groups, local, 0)

    dec_copy.wait_recv()

    def spread_decay(g, _):
        rows = pl.ds(pl.multiple_of(g * per, per), per)
        pdec_x[pl.ds(pl.multiple_of(g * gw, gw), gw), :] = exact(spread, pdecs[rows, :], TN)
        return 0

    lax.fori_loop(0, groups, spread_decay, 0)

    @pl.when(first_pair)
    def _():
        ebuf[...] = state_ref[...]

    @pl.when(last_pair)
    def _():
        gbuf[...] = jnp.zeros_like(gbuf)

    def ordered(here, there):
        return jnp.where(left, here, there), jnp.where(left, there, here)

    def forward(m, _):
        k = mine(m)
        rows = piece(k)
        summary_copy(k).wait_recv()

        @pl.when(jnp.logical_not(first_pair))
        def _():
            forward_copy(k).wait_recv()

        decay_a, decay_b = ordered(dec_x[rows, :], pdec_x[rows, :])
        sum_a, sum_b = ordered(summ[rows, :], psum[rows, :])
        enter = ebuf[rows, :]
        middle = decay_a * enter + sum_a

        @pl.when(jnp.logical_not(last_pair))
        def _():
            f_out[rows, :] = decay_b * middle + sum_b
            forward_copy(k).start()

        ent[rows, :], f_other[rows, :] = ordered(enter, middle)
        enter_copy(k).start()
        return 0

    def backward(m, _):
        k = mine(m)
        rows = piece(k)
        grad_out_copy(k).wait_recv()

        @pl.when(jnp.logical_not(last_pair))
        def _():
            backward_copy(k).wait_recv()

        decay_a, decay_b = ordered(dec_x[rows, :], pdec_x[rows, :])
        grad_a, grad_b = ordered(d_ent[rows, :], pd_ent[rows, :])
        leave = gbuf[rows, :]
        middle = decay_b * leave + grad_b

        @pl.when(jnp.logical_not(first_pair))
        def _():
            b_out[rows, :] = decay_a * middle + grad_a
            backward_copy(k).start()

        d_exi[rows, :], b_other[rows, :] = ordered(middle, leave)
        exit_copy(k).start()
        return 0

    lax.fori_loop(0, jnp.where(last_pair, half, own), forward, 0)

    def output(g, _):
        at, nat, hat = (pl.multiple_of(g * w, w) for w in (gw, nn, per))
        cols, ncols, rows = pl.ds(at, gw), pl.ds(nat, nn), pl.ds(hat, per)

        @pl.when(last_pair & (g < groups - 1))
        def _():
            lax.fori_loop((g + 1) * half, (g + 2) * half, forward, 0)

        for i in range(half):
            enter_copy(theirs(g * half + i)).wait_recv()
        bs, cs = split(bco[:, ncols]), split(cco[:, ncols])
        scores = dot3(cs, bs, NT)
        scores_t = dot3(bs, cs, NT)
        ents = split(ent[pl.ds(at, gw), :])
        s = sig[:, cols]
        sc = step_x[:, cols] * s
        cum, cum_c = cum_row[rows, :], cum_t[g]
        within = []
        for j in range(blocks):
            sc4 = sc[:, j * bw : (j + 1) * bw]
            ms, rs = [], []
            for i in range(BLOCK):
                h = j * BLOCK + i
                gap = cum_c[:, h : h + 1] - cum[h : h + 1, :]
                mask = jnp.exp(jnp.where(lower, gap, -1e30))
                mask_s[h] = mask
                ms.append(split(scores * mask))
                rs.append(split(jnp.where(lane_of == i, sc4, 0.0)))
            m = tuple(jnp.concatenate([v[q] for v in ms], axis=1) for q in (0, 1))
            r = tuple(jnp.concatenate([v[q] for v in rs], axis=0) for q in (0, 1))
            within.append(dot3(m, r, NN))
        inner = jnp.concatenate(within, axis=1) + ecum_x[:, cols] * dot3(cs, ents, NT)
        skx = jnp.sum(spread * skcol[rows, 0:1], axis=0, keepdims=True)
        mixed = inner + skx * s
        z = z_ref[:, cols].astype(F32)
        zs = sigmoid(z)
        sz = z * zs
        gated = mixed * sz
        inv = lax.rsqrt(jnp.mean(gated * gated, axis=1, keepdims=True) + EPS)
        dn = go_ref[:, cols].astype(F32) * gain_ref[:, cols]
        unit = gated * inv
        dg = inv * (dn - unit * jnp.mean(dn * unit, axis=1, keepdims=True))
        gz_ref[:, cols] = (dg * mixed * (zs + sz * (1.0 - zs))).astype(BF16)
        dm = dg * sz
        dm_s[:, cols] = dm
        r1_s[rows, :] = sum(dot(spread_b, v, NT) for v in split(dm * inner))
        dcar = split(dm * ecum_x[:, cols])
        d_ent[pl.ds(at, gw), :] = dot3(dcar, cs, TN)
        for i in range(half):
            grad_out_copy(theirs(g * half + i)).start()

        @pl.when(last_pair & (g > 0))
        def _():
            lax.fori_loop((g - 1) * half, g * half, backward, 0)

        ds = jnp.zeros((tok, tok), F32)
        for j in range(blocks):
            dm4 = dm[:, j * bw : (j + 1) * bw]
            scs = split(sc[:, j * bw : (j + 1) * bw])
            ms, rs = [], []
            for i in range(BLOCK):
                h = j * BLOCK + i
                gap = cum[h : h + 1, :] - cum_c[:, h : h + 1]
                ms.append(split(scores_t * jnp.exp(jnp.where(upper, gap, -1e30))))
                rs.append(split(jnp.where(lane_of == i, dm4, 0.0)))
                ds = ds + dot3(rs[-1], scs, NT) * mask_s[h]
            m = tuple(jnp.concatenate([v[q] for v in ms], axis=1) for q in (0, 1))
            r = tuple(jnp.concatenate([v[q] for v in rs], axis=0) for q in (0, 1))
            dsc_s[:, pl.ds(at + j * bw, bw)] = dot3(m, r, NN)
        dss = split(ds)
        dcs[:, ncols] = dot3(dss, bs, NN) + dot3(dcar, ents, NN)
        dbs[:, ncols] = dot3(dss, cs, TN)
        return 0

    lax.fori_loop(0, groups, output, 0)

    lax.fori_loop(
        jnp.where(last_pair, own - half, 0), jnp.where(first_pair, half, own), backward, 0
    )
    from_t = (iota((tok, tok), 0) >= iota((tok, tok), 1)).astype(F32)

    def grad_copy(g):
        return remote(gsend.at[g], ghalo.at[g], gs_sem.at[g], gr_sem.at[g], before)

    def silu_back(grad, pre):
        s = sigmoid(pre)
        return grad * (s + pre * s * (1.0 - s))

    def closing(g, _):
        at, nat, hat = (pl.multiple_of(g * w, w) for w in (gw, nn, per))
        cols, ncols, rows = pl.ds(at, gw), pl.ds(nat, nn), pl.ds(hat, per)

        @pl.when(first_pair & (g < groups - 1))
        def _():
            lax.fori_loop((g + 1) * half, (g + 2) * half, backward, 0)

        for i in range(half):
            exit_copy(theirs(g * half + i)).wait_recv()

        grad = d_exi[pl.ds(at, gw), :]
        grads = split(grad)
        s, sx, ex = sig[:, cols], step_x[:, cols], e_x[:, cols]
        bs = split(bco[:, ncols])
        both = dsc_s[:, cols] + ex * dot3(bs, grads, NT)
        skx = jnp.sum(spread * skcol[rows, 0:1], axis=0, keepdims=True)
        gpx = silu_back(sx * both + skx * dm_s[:, cols], pre_x[:, cols])
        db = dbs[:, ncols] + dot3(split(s * sx * ex), grads, NN)
        gpbv = silu_back(db, pre_b[:, ncols])
        gpcv = silu_back(dcs[:, ncols], pre_c[:, ncols])
        gp[0:tok, cols] = gpx
        gpb[g, 0:tok, 0:nn] = gpbv
        gpb[g, 0:tok, nn : 2 * nn] = gpcv

        @pl.when(jnp.logical_not(first))
        def _():
            gsend[g, :, 0:gw] = gpx[0:8]
            gsend[g, :, gw : gw + nn] = gpbv[0:8]
            gsend[g, :, gw + nn :] = gpcv[0:8]
            grad_copy(g).start()

        u = sum(dot(spread_b, v, NT) for v in split(s * both))
        hrows = pl.ds(at, gw)
        leave = dec_x[hrows, :] * ent[hrows, :] + summ[hrows, :]
        lane = jnp.sum(exact(spread, grad * leave), axis=1, keepdims=True)
        st = step_row[rows, :]
        d_rate = exact(r1_s[rows, :] - st * u, from_t) + lane
        gdt_ref[rows, :] = (u - acol[rows, :] * d_rate) * sigmoid(dt_ref[rows, :])
        return 0

    lax.fori_loop(0, groups, closing, 0)

    @pl.when(last)
    def _():
        ghalo[...] = jnp.zeros_like(ghalo)

    def finish(g, _):
        at, nat = (pl.multiple_of(g * w, w) for w in (gw, nn))
        cols, ncols = pl.ds(at, gw), pl.ds(nat, nn)

        @pl.when(jnp.logical_not(last))
        def _():
            grad_copy(g).wait_recv()

        gp[tok : tok + 8, cols] = ghalo[g, :, 0:gw]
        gpb[g, tok : tok + 8, :] = ghalo[g, :, gw:]
        tx = tb = tc = 0.0
        for k in range(taps):
            row = slice(taps - 1 - k, taps - 1 - k + tok)
            tx = tx + wx_ref[k : k + 1, cols] * gp[row, cols]
            tb = tb + wb_ref[k : k + 1, ncols] * gpb[g, row, 0:nn]
            tc = tc + wc_ref[k : k + 1, ncols] * gpb[g, row, nn : 2 * nn]
        gx_ref[:, cols] = tx.astype(BF16)
        gb_ref[:, ncols] = tb.astype(BF16)
        gc_ref[:, ncols] = tc.astype(BF16)
        return 0

    lax.fori_loop(0, groups, finish, 0)

    dec_copy.wait_send()

    def drain(m, _):
        summary_copy(theirs(m)).wait_send()
        grad_out_copy(theirs(m)).wait_send()
        enter_copy(mine(m)).wait_send()
        exit_copy(mine(m)).wait_send()

        @pl.when(jnp.logical_not(last_pair))
        def _():
            forward_copy(mine(m)).wait_send()

        @pl.when(jnp.logical_not(first_pair))
        def _():
            backward_copy(mine(m)).wait_send()

        return 0

    lax.fori_loop(0, own, drain, 0)

    @pl.when(jnp.logical_not(last))
    def _():
        for copy in halos:
            copy.wait_send()

    @pl.when(jnp.logical_not(first))
    def _():
        def drain_halo(g, _):
            grad_copy(g).wait_send()
            return 0

        lax.fori_loop(0, groups, drain_halo, 0)


def write_out(*refs):
    count = len(refs) // 2
    for src, dst in zip(refs[:count], refs[count:]):
        dst[...] = src[...]


def per_device(
    x_stream, z_stream, b_stream, c_stream, dt_raw, a_log, skip_coef, conv_x, conv_b, conv_c, norm_gain, state_in, grad_out
):
    tok, chan = x_stream.shape
    heads, hd, nn = state_in.shape
    wide = b_stream.shape[1]
    groups = wide // nn
    per, gw = heads // groups, chan // groups
    chunks = chan // (PIECE * hd)
    dma = pltpu.SemaphoreType.DMA

    def v(*shape, dtype=F32):
        return pltpu.VMEM(shape, dtype)

    scratch = [
        v(16, chan, dtype=BF16), v(16, wide, dtype=BF16), v(16, wide, dtype=BF16),
        v(tok + 8, gw), v(tok, chan), v(tok, wide), v(tok, wide), v(tok, chan), v(tok, wide), v(tok, wide),
        v(heads, tok), v(heads, tok), v(heads, 128), v(heads, 128), v(groups, tok, 128),
        v(tok, chan), v(tok, chan), v(tok, chan), v(chan, nn), v(chan, nn), v(heads, 128), v(heads, 128),
        *([v(chan, nn)] * 12),
        v(tok, chan), v(heads, tok), v(tok, chan), v(tok, wide), v(tok, wide), v(per, tok, tok),
        v(tok + 8, chan), v(groups, 8, gw + 2 * nn), v(groups, 8, gw + 2 * nn), v(groups, tok + 8, 2 * nn),
        dma((4,)), dma((4,)), dma((6, 2, chunks)), dma((groups,)), dma((groups,)),
    ]
    vmem = pl.BlockSpec(memory_space=pltpu.VMEM)
    outs = [
        jax.ShapeDtypeStruct(a.shape, a.dtype) for a in (x_stream, z_stream, b_stream, c_stream, dt_raw)
    ]
    results = pl.pallas_call(
        kernel,
        out_shape=outs,
        in_specs=[vmem] * 13,
        out_specs=[vmem] * 5,
        scratch_shapes=scratch,
        compiler_params=pltpu.CompilerParams(
            collective_id=0, has_side_effects=True, vmem_limit_bytes=56 * 2**20
        ),
    )(
        x_stream, z_stream, b_stream, c_stream, dt_raw, a_log.reshape(1, heads), skip_coef.reshape(1, heads),
        conv_x, conv_b, conv_c, norm_gain.reshape(1, chan), state_in.reshape(heads * hd, nn), grad_out,
    )
    return pl.pallas_call(write_out, out_shape=outs, in_specs=[vmem] * 5, out_specs=[vmem] * 5)(*results)


def solution(mesh):
    rows = P(("group", "seq"), "head")
    turned = P("head", ("group", "seq"))
    taps = P(None, "head")
    return jax.shard_map(
        per_device,
        mesh=mesh,
        in_specs=(
            rows, rows, rows, rows, turned, P(("group", "head")), P("head"), taps, taps, taps, P("head"),
            P(("group", "head"), None, None), rows,
        ),
        out_specs=(rows, rows, rows, rows, turned),
        check_vma=False,
    )
```
